512 devices in a mesh: pts: 128 (over y, x, z_hi), band: 4 (over z_lo, core).
Axes of the slice: x: 4, y: 8, z: 8 (z_hi: 4, z_lo: 2; z = z_hi * 2 + z_lo), core: 2. Of those that a mesh axis runs over, the one named last changes fastest.
Arguments:
- orbitals: bfloat16 [2000, 32768], P('band', 'pts'), may hold values from -6 to 6
- partner: int32 [128], P('pts'), may hold values from 0 to 127, as said below
- self_kernel: bfloat16 [32768, 256], P('pts'), may hold values from -0.005859375 to 0.005859375
- pair_kernel: bfloat16 [32768, 256], P('pts'), may hold values from -0.005859375 to 0.005859375
Outputs:
- exchange_out: bfloat16 [2000, 32768], P('band', 'pts')
The draws below stay inside these ranges and needn't reach their ends.
Inputs may be any that keep to these rules, and one draw needn't show every extreme that they name: partner[p] = (r - p) mod the number of point blocks, for one odd round number r drawn per run; so blocks pair off, and none is its own partner.
All inputs are finite; a program needn't handle non-finite values.
Results may differ from the reference program's by a relative error of at most 0.017.
Values may be sent and summed in bfloat16 or wider, within the bound.
A program may use at most 64 MiB of HBM per device.

```python
import jax
import jax.numpy as jnp
from jax import lax

BANDS = 2000
BLK = 256
POINTS = 32768
N_PTS = 128
N_BAND = 4


def draw_partner(key, part):
    key = jax.random.fold_in(key, 7)
    halfway = jax.random.randint(key, (), 0, N_PTS // 2)
    round_number = 2 * halfway + 1
    return ((round_number - jnp.arange(N_PTS, dtype=jnp.int32)) % N_PTS).astype(jnp.int32)


def block_levels(own_key, shape, pieces, smallest, largest):
    loudness = 1.0
    for axis_at, parts in pieces:
        draws = jax.random.uniform(jax.random.fold_in(jax.random.fold_in(own_key, 6), axis_at), (parts,), jnp.float32, smallest / len(pieces), largest / len(pieces))
        loudness = loudness * jnp.repeat(jnp.exp(draws), shape[axis_at] // parts).reshape((-1,) + (1,) * (len(shape) - 1 - axis_at))
    return loudness


def gaussian(key, shape, deviation, reach, split=(), kind=jnp.bfloat16):
    result = jax.random.normal(key, shape, jnp.float32) * deviation
    if len(split) > 0:
        result = block_levels(key, shape, split, -0.22, 0.18) * result
    return jnp.clip(result, min=-reach, max=reach).astype(kind)


def setup_inputs(seed: int = 0) -> dict:
    seeds = jax.random.split(jax.random.key(seed), 5)
    return {
        "orbitals": gaussian(seeds[0], (BANDS, POINTS), 1.0, 6.0, ((0, 4), (1, 128))),
        "partner": draw_partner(jax.random.fold_in(seeds[4], 71), 0),
        "self_kernel": gaussian(seeds[2], (POINTS, BLK), (2 * BLK * BANDS) ** -0.5, 0.005859375, ((0, 128),)),
        "pair_kernel": gaussian(seeds[3], (POINTS, BLK), (2 * BLK * BANDS) ** -0.5, 0.005859375, ((0, 128),)),
    }


def reference(orbitals, partner, self_kernel, pair_kernel):
    group_bands = BANDS // N_BAND

    def one_block(block_id):
        own_block = lax.dynamic_slice_in_dim(orbitals, block_id * BLK, BLK, 1)
        partner_block = lax.dynamic_slice_in_dim(orbitals, partner[block_id] * BLK, BLK, 1)
        stacked = jnp.concatenate([own_block, partner_block], axis=1)
        grouped_own = own_block.reshape(N_BAND, group_bands, BLK).astype(jnp.float32)
        grouped_pair = stacked.reshape(N_BAND, group_bands, 2 * BLK).astype(jnp.float32)
        partials = jnp.einsum('gbm,gbn->gmn', grouped_own, grouped_pair).astype(jnp.bfloat16)
        partials = lax.optimization_barrier(partials)
        density = jnp.sum(partials.astype(jnp.float32), axis=0)
        kernel = jnp.concatenate([lax.dynamic_slice_in_dim(self_kernel, block_id * BLK, BLK, 0),
                                  lax.dynamic_slice_in_dim(pair_kernel, block_id * BLK, BLK, 0)], axis=1)
        weights = (kernel.astype(jnp.float32) * density).astype(jnp.bfloat16)
        return jnp.dot(stacked, weights.T, preferred_element_type=jnp.float32).astype(jnp.bfloat16)

    blocks = lax.map(one_block, jnp.arange(N_PTS, dtype=jnp.int32))
    return jnp.transpose(blocks, (1, 0, 2)).reshape(BANDS, BLK * N_PTS)
```

```python
import functools

import jax
import jax.numpy as jnp
from jax import lax
from jax.experimental import pallas as pl
from jax.experimental.pallas import tpu as pltpu
from jax.sharding import PartitionSpec as P

MESH = pl.DeviceIdType.MESH
HALVES = 2


def fused(
    round_number,
    blocks,
    groups,
    orbitals,
    self_kernel,
    pair_kernel,
    out,
    own,
    arrived,
    kernels,
    own_t,
    part_self,
    part_pair,
    got_self,
    got_pair,
    dens_self,
    dens_pair,
    total,
    local_sem,
    swap_send,
    swap_recv,
    rs_send,
    rs_recv,
    ag_send,
    ag_recv,
):
    me = lax.axis_index("pts")
    band = lax.axis_index("band")
    partner = lax.rem(round_number - me + blocks, blocks)
    peers = [lax.rem(band + d, groups) for d in range(1, groups)]
    sources = [lax.rem(band + groups - d, groups) for d in range(1, groups)]
    points = own.shape[1]
    width = points // HALVES

    loads = [
        pltpu.make_async_copy(orbitals, own, local_sem.at[0]),
        pltpu.make_async_copy(self_kernel, kernels.at[0], local_sem.at[1]),
        pltpu.make_async_copy(pair_kernel, kernels.at[1], local_sem.at[2]),
    ]
    for load in loads:
        load.start()

    barrier = pltpu.get_barrier_semaphore()
    pl.semaphore_signal(barrier, inc=1, device_id=(partner, band), device_id_type=MESH)
    for peer in peers:
        pl.semaphore_signal(barrier, inc=1, device_id=(me, peer), device_id_type=MESH)
    pl.semaphore_wait(barrier, groups)

    swaps = []
    for h in range(HALVES):
        columns = pl.ds(h * width, width)
        swap = pltpu.make_async_remote_copy(
            src_ref=orbitals.at[:, columns],
            dst_ref=arrived.at[:, columns],
            send_sem=swap_send.at[h],
            recv_sem=swap_recv.at[h],
            device_id=(partner, band),
            device_id_type=MESH,
        )
        swap.start()
        swaps.append(swap)

    pending = []

    def scatter(stage, part, got, product):
        rows = part.shape[1]
        for k in range(groups):
            part[k] = product[k * rows : (k + 1) * rows].astype(jnp.bfloat16)
        copies = []
        for d in range(groups - 1):
            copy = pltpu.make_async_remote_copy(
                src_ref=part.at[peers[d]],
                dst_ref=got.at[d],
                send_sem=rs_send.at[stage, d],
                recv_sem=rs_recv.at[stage, d],
                device_id=(me, peers[d]),
                device_id_type=MESH,
            )
            copy.start()
            copies.append(copy)
        pending.extend(copies)
        return copies

    def gather(stage, part, got, dens, arriving):
        value = part[band].astype(jnp.float32)
        for d, copy in enumerate(arriving):
            copy.wait_recv()
            value = value + got[d].astype(jnp.float32)
        dens[band] = value.astype(jnp.bfloat16)
        copies = []
        for d in range(groups - 1):
            copy = pltpu.make_async_remote_copy(
                src_ref=dens.at[band],
                dst_ref=dens.at[band],
                send_sem=ag_send.at[stage, d],
                recv_sem=ag_recv.at[stage, d],
                device_id=(me, peers[d]),
                device_id_type=MESH,
            )
            copy.start()
            copies.append(copy)
        pending.extend(copies)
        return copies

    def weights(kernel, dens, arriving):
        for copy in arriving:
            copy.wait_recv()
        density = dens[...].reshape(points, -1).astype(jnp.float32)
        return (kernel.astype(jnp.float32) * density).astype(jnp.bfloat16)

    def apply(block, weight):
        return lax.dot_general(
            block, weight, (((1,), (1,)), ((), ())), preferred_element_type=jnp.float32
        )

    loads[0].wait()
    own_t[...] = own[...].T
    product = jnp.dot(own_t[...], own[...], preferred_element_type=jnp.float32)
    copies = scatter(0, part_self, got_self, product)
    copies = gather(0, part_self, got_self, dens_self, copies)
    loads[1].wait()
    loads[2].wait()
    total[...] = apply(own[...], weights(kernels[0], dens_self, copies))

    for h in range(HALVES):
        columns = pl.ds(h * width, width)
        swaps[h].wait_recv()
        product = jnp.dot(own_t[...], arrived[:, columns], preferred_element_type=jnp.float32)
        copies = scatter(1 + h, part_pair.at[h], got_pair.at[h], product)
        copies = gather(1 + h, part_pair.at[h], got_pair.at[h], dens_pair.at[h], copies)
        weight = weights(kernels[1, :, columns], dens_pair.at[h], copies)
        value = total[...] + apply(arrived[:, columns], weight)
        if h + 1 < HALVES:
            total[...] = value
        else:
            out[...] = value.astype(out.dtype)

    for copy in swaps + pending:
        copy.wait_send()


def exchange(round_number, blocks, groups, orbitals, self_kernel, pair_kernel):
    bands, points = orbitals.shape
    rows, width = points // groups, points // HALVES
    half = jnp.bfloat16
    dma = pltpu.SemaphoreType.DMA
    return pl.pallas_call(
        functools.partial(fused, round_number, blocks, groups),
        out_shape=jax.ShapeDtypeStruct((bands, points), half),
        in_specs=[pl.BlockSpec(memory_space=pl.ANY)] * 3,
        out_specs=pl.BlockSpec(memory_space=pltpu.VMEM),
        scratch_shapes=[
            pltpu.VMEM((bands, points), half),
            pltpu.VMEM((bands, points), half),
            pltpu.VMEM((2, points, points), half),
            pltpu.VMEM((points, bands), half),
            pltpu.VMEM((groups, rows, points), half),
            pltpu.VMEM((HALVES, groups, rows, width), half),
            pltpu.VMEM((groups - 1, rows, points), half),
            pltpu.VMEM((HALVES, groups - 1, rows, width), half),
            pltpu.VMEM((groups, rows, points), half),
            pltpu.VMEM((HALVES, groups, rows, width), half),
            pltpu.VMEM((bands, points), jnp.float32),
            dma((3,)),
            dma((HALVES,)),
            dma((HALVES,)),
            dma((1 + HALVES, groups - 1)),
            dma((1 + HALVES, groups - 1)),
            dma((1 + HALVES, groups - 1)),
            dma((1 + HALVES, groups - 1)),
        ],
        compiler_params=pltpu.CompilerParams(
            collective_id=round_number // 2,
            has_side_effects=True,
            vmem_limit_bytes=32 * 1024 * 1024,
        ),
    )(orbitals, self_kernel, pair_kernel)


def per_device(blocks, groups, orbitals, partner, self_kernel, pair_kernel):
    round_number = lax.rem(partner[0] + lax.axis_index("pts"), blocks)
    rounds = [
        functools.partial(exchange, 2 * k + 1, blocks, groups) for k in range(blocks // 2)
    ]
    return lax.switch(round_number // 2, rounds, orbitals, self_kernel, pair_kernel)


def solution(mesh):
    return jax.shard_map(
        functools.partial(per_device, mesh.shape["pts"], mesh.shape["band"]),
        mesh=mesh,
        in_specs=(P("band", "pts"), P("pts"), P("pts", None), P("pts", None)),
        out_specs=P("band", "pts"),
        check_vma=False,
    )
```

```python
import functools

import jax
import jax.numpy as jnp
from jax import lax
from jax.experimental import pallas as pl
from jax.experimental.pallas import tpu as pltpu
from jax.sharding import PartitionSpec as P

MESH = pl.DeviceIdType.MESH
VMEM = 56 * 1024 * 1024


def swap_kernel(round_number, blocks, orbitals, arrived, send_sem, recv_sem):
    partner = {"pts": lax.rem(round_number + blocks - lax.axis_index("pts"), blocks)}
    barrier = pltpu.get_barrier_semaphore()
    pl.semaphore_signal(barrier, inc=1, device_id=partner, device_id_type=MESH)
    pl.semaphore_wait(barrier, 1)
    copy = pltpu.make_async_remote_copy(
        src_ref=orbitals,
        dst_ref=arrived,
        send_sem=send_sem,
        recv_sem=recv_sem,
        device_id=partner,
        device_id_type=MESH,
    )
    copy.start()
    copy.wait()


def swap(round_number, collective, blocks, orbitals):
    return pl.pallas_call(
        functools.partial(swap_kernel, round_number, blocks),
        out_shape=jax.ShapeDtypeStruct(orbitals.shape, orbitals.dtype),
        in_specs=[pl.BlockSpec(memory_space=pl.ANY)],
        out_specs=pl.BlockSpec(memory_space=pl.ANY),
        scratch_shapes=[pltpu.SemaphoreType.DMA, pltpu.SemaphoreType.DMA],
        compiler_params=pltpu.CompilerParams(
            collective_id=collective, has_side_effects=True, vmem_limit_bytes=VMEM
        ),
    )(orbitals)


def finish_kernel(
    shift,
    blocks,
    groups,
    orbitals,
    swapped,
    self_kernel,
    pair_kernel,
    out,
    own,
    arrived,
    kernels,
    own_t,
    part,
    got,
    dens,
    total,
    local_sem,
    shift_sem,
    rs_send,
    rs_recv,
    ag_send,
    ag_recv,
):
    me = lax.axis_index("pts")
    band = lax.axis_index("band")
    peers = [lax.rem(band + d, groups) for d in range(1, groups)]
    points = own.shape[1]
    rows = points // groups

    loads = [
        pltpu.make_async_copy(orbitals, own, local_sem.at[0]),
        pltpu.make_async_copy(self_kernel, kernels.at[0], local_sem.at[1]),
        pltpu.make_async_copy(pair_kernel, kernels.at[1], local_sem.at[2]),
    ]
    if not shift:
        loads.append(pltpu.make_async_copy(swapped, arrived, local_sem.at[3]))
    for load in loads:
        load.start()

    barrier = pltpu.get_barrier_semaphore()
    for peer in peers:
        pl.semaphore_signal(barrier, inc=1, device_id={"band": peer}, device_id_type=MESH)
    if shift:
        source = {"pts": lax.rem(me + blocks - shift, blocks)}
        pl.semaphore_signal(barrier, inc=1, device_id=source, device_id_type=MESH)
    pl.semaphore_wait(barrier, groups if shift else groups - 1)
    if shift:
        moved = pltpu.make_async_remote_copy(
            src_ref=swapped,
            dst_ref=arrived,
            send_sem=shift_sem.at[0],
            recv_sem=shift_sem.at[1],
            device_id={"pts": lax.rem(me + shift, blocks)},
            device_id_type=MESH,
        )
        moved.start()

    pending = []

    def scatter(stage, block):
        product = jnp.dot(own_t[...], block[...], preferred_element_type=jnp.float32)
        for k in range(groups):
            part[stage, k] = product[k * rows : (k + 1) * rows].astype(jnp.bfloat16)
        copies = []
        for d in range(groups - 1):
            copy = pltpu.make_async_remote_copy(
                src_ref=part.at[stage, peers[d]],
                dst_ref=got.at[stage, d],
                send_sem=rs_send.at[stage, d],
                recv_sem=rs_recv.at[stage, d],
                device_id={"band": peers[d]},
                device_id_type=MESH,
            )
            copy.start()
            copies.append(copy)
        pending.extend(copies)
        return copies

    def gather(stage, arriving):
        value = part[stage, band].astype(jnp.float32)
        for d, copy in enumerate(arriving):
            copy.wait_recv()
            value = value + got[stage, d].astype(jnp.float32)
        dens[stage, band] = value.astype(jnp.bfloat16)
        copies = []
        for d in range(groups - 1):
            copy = pltpu.make_async_remote_copy(
                src_ref=dens.at[stage, band],
                dst_ref=dens.at[stage, band],
                send_sem=ag_send.at[stage, d],
                recv_sem=ag_recv.at[stage, d],
                device_id={"band": peers[d]},
                device_id_type=MESH,
            )
            copy.start()
            copies.append(copy)
        pending.extend(copies)
        return copies

    def apply(stage, block, arriving):
        for copy in arriving:
            copy.wait_recv()
        density = dens[stage].reshape(points, points).astype(jnp.float32)
        weight = (kernels[stage].astype(jnp.float32) * density).astype(jnp.bfloat16)
        return lax.dot_general(
            block[...], weight, (((1,), (1,)), ((), ())), preferred_element_type=jnp.float32
        )

    loads[0].wait()
    own_t[...] = own[...].T
    first = scatter(0, own)
    if shift:
        first = gather(0, first)
        moved.wait_recv()
        second = scatter(1, arrived)
    else:
        loads[3].wait()
        second = scatter(1, arrived)
        first = gather(0, first)
    loads[1].wait()
    loads[2].wait()
    if shift:
        total[...] = apply(0, own, first)
        second = gather(1, second)
    else:
        second = gather(1, second)
        total[...] = apply(0, own, first)
    out[...] = (total[...] + apply(1, arrived, second)).astype(out.dtype)

    if shift:
        moved.wait_send()
    for copy in pending:
        copy.wait_send()


def finish(shift, collective, blocks, groups, orbitals, swapped, self_kernel, pair_kernel):
    bands, points = orbitals.shape
    rows = points // groups
    half = jnp.bfloat16
    dma = pltpu.SemaphoreType.DMA
    return pl.pallas_call(
        functools.partial(finish_kernel, shift, blocks, groups),
        out_shape=jax.ShapeDtypeStruct((bands, points), half),
        in_specs=[pl.BlockSpec(memory_space=pl.ANY)] * 4,
        out_specs=pl.BlockSpec(memory_space=pltpu.VMEM),
        scratch_shapes=[
            pltpu.VMEM((bands, points), half),
            pltpu.VMEM((bands, points), half),
            pltpu.VMEM((2, points, points), half),
            pltpu.VMEM((points, bands), half),
            pltpu.VMEM((2, groups, rows, points), half),
            pltpu.VMEM((2, groups - 1, rows, points), half),
            pltpu.VMEM((2, groups, rows, points), half),
            pltpu.VMEM((bands, points), jnp.float32),
            dma((4,)),
            dma((2,)),
            dma((2, groups - 1)),
            dma((2, groups - 1)),
            dma((2, groups - 1)),
            dma((2, groups - 1)),
        ],
        compiler_params=pltpu.CompilerParams(
            collective_id=collective, has_side_effects=True, vmem_limit_bytes=VMEM
        ),
    )(orbitals, swapped, self_kernel, pair_kernel)


def per_device(blocks, groups, orbitals, partner, self_kernel, pair_kernel):
    shift = max(blocks // 16, 2)
    pairs = shift // 2
    count = blocks // 4
    round_number = lax.rem(partner[0] + lax.axis_index("pts"), blocks)
    bit = lax.rem(round_number // shift, 2)
    index = round_number // (2 * shift) * pairs + lax.rem(round_number, shift) // 2
    swaps = [
        functools.partial(swap, 2 * shift * (k // pairs) + 2 * (k % pairs) + 1, k, blocks)
        for k in range(count)
    ]
    swapped = lax.switch(index, swaps, orbitals)
    return lax.cond(
        bit == 1,
        functools.partial(finish, shift, count, blocks, groups),
        functools.partial(finish, 0, count + 1, blocks, groups),
        orbitals,
        swapped,
        self_kernel,
        pair_kernel,
    )


def solution(mesh):
    return jax.shard_map(
        functools.partial(per_device, mesh.shape["pts"], mesh.shape["band"]),
        mesh=mesh,
        in_specs=(P("band", "pts"), P("pts"), P("pts", None), P("pts", None)),
        out_specs=P("band", "pts"),
        check_vma=False,
    )
```

```python
import functools

import jax
import jax.numpy as jnp
from jax import lax
from jax.experimental import pallas as pl
from jax.experimental.pallas import tpu as pltpu
from jax.sharding import PartitionSpec as P

MESH = pl.DeviceIdType.MESH
VMEM = 56 * 1024 * 1024


def swap_kernel(round_number, blocks, orbitals, arrived, between, send_sem, recv_sem):
    me = lax.axis_index("pts")
    line = max(blocks // 8, 2)
    partner = lax.rem(round_number + blocks - me, blocks)
    row_mate = partner // line * line + lax.rem(me, line)
    place_mate = me // line * line + lax.rem(partner, line)
    moves = row_mate != me
    bands, points = orbitals.shape
    split = bands // 32 * 16
    width = points // 2
    pieces = [
        (pl.ds(first, size), pl.ds(column * width, width))
        for first, size in ((0, split), (split, bands - split))
        for column in range(2)
    ]
    mates = [row_mate, place_mate, row_mate, place_mate]

    barrier = pltpu.get_barrier_semaphore()
    pl.semaphore_signal(barrier, inc=1, device_id={"pts": place_mate}, device_id_type=MESH)

    @pl.when(moves)
    def _():
        pl.semaphore_signal(barrier, inc=1, device_id={"pts": row_mate}, device_id_type=MESH)

    def send(src, dst, piece, semaphore, mate):
        return pltpu.make_async_remote_copy(
            src_ref=src.at[piece],
            dst_ref=dst.at[piece],
            send_sem=send_sem.at[semaphore],
            recv_sem=recv_sem.at[semaphore],
            device_id={"pts": mate},
            device_id_type=MESH,
        )

    count = len(pieces)

    @pl.when(jnp.logical_not(moves))
    def _():
        pl.semaphore_wait(barrier, 1)
        copies = [
            send(orbitals, arrived, piece, count + k, place_mate) for k, piece in enumerate(pieces)
        ]
        for copy in copies:
            copy.start()
        for copy in copies:
            copy.wait()

    @pl.when(moves)
    def _():
        pl.semaphore_wait(barrier, 2)
        firsts = [
            send(orbitals, between, piece, k, mates[k]) for k, piece in enumerate(pieces)
        ]
        seconds = [
            send(between, arrived, piece, count + k, mates[k ^ 1]) for k, piece in enumerate(pieces)
        ]
        for copy in firsts:
            copy.start()
        for first, second in zip(firsts, seconds):
            first.wait_recv()
            second.start()
        for copy in firsts:
            copy.wait_send()
        for copy in seconds:
            copy.wait()


def swap(round_number, collective, blocks, orbitals):
    return pl.pallas_call(
        functools.partial(swap_kernel, round_number, blocks),
        out_shape=jax.ShapeDtypeStruct(orbitals.shape, orbitals.dtype),
        in_specs=[pl.BlockSpec(memory_space=pl.ANY)],
        out_specs=pl.BlockSpec(memory_space=pl.ANY),
        scratch_shapes=[
            pltpu.VMEM(orbitals.shape, orbitals.dtype),
            pltpu.SemaphoreType.DMA((8,)),
            pltpu.SemaphoreType.DMA((8,)),
        ],
        compiler_params=pltpu.CompilerParams(
            collective_id=collective, has_side_effects=True, vmem_limit_bytes=VMEM
        ),
    )(orbitals)


def finish_kernel(
    shift,
    blocks,
    groups,
    orbitals,
    swapped,
    self_kernel,
    pair_kernel,
    out,
    own,
    arrived,
    kernels,
    own_t,
    part,
    part_in,
    chip,
    chip_in,
    dens,
    total,
    local_sem,
    shift_sem,
    chip_send,
    chip_recv,
    link_send,
    link_recv,
    back_send,
    back_recv,
):
    me = lax.axis_index("pts")
    band = lax.axis_index("band")
    core = lax.rem(band, 2)
    sibling = {"band": band + 1 - 2 * core}
    across = {"band": lax.rem(band + 2, groups)}
    points = own.shape[1]
    rows = points // 2

    loads = [
        pltpu.make_async_copy(orbitals, own, local_sem.at[0]),
        pltpu.make_async_copy(self_kernel, kernels.at[0], local_sem.at[1]),
        pltpu.make_async_copy(pair_kernel, kernels.at[1], local_sem.at[2]),
    ]
    if not shift:
        loads.append(pltpu.make_async_copy(swapped, arrived, local_sem.at[3]))
    for load in loads:
        load.start()

    barrier = pltpu.get_barrier_semaphore()
    pl.semaphore_signal(barrier, inc=1, device_id=sibling, device_id_type=MESH)
    pl.semaphore_signal(barrier, inc=1, device_id=across, device_id_type=MESH)
    if shift:
        source = {"pts": lax.rem(me + blocks - shift, blocks)}
        pl.semaphore_signal(barrier, inc=1, device_id=source, device_id_type=MESH)
    pl.semaphore_wait(barrier, 3 if shift else 2)

    pending = []

    def send(src, dst, semaphores, target):
        copy = pltpu.make_async_remote_copy(
            src_ref=src,
            dst_ref=dst,
            send_sem=semaphores[0],
            recv_sem=semaphores[1],
            device_id=target,
            device_id_type=MESH,
        )
        copy.start()
        pending.append(copy)
        return copy

    def wide(value):
        return value.astype(jnp.float32)

    def narrow(value):
        return value.astype(jnp.bfloat16)

    def partial(stage, block):
        product = jnp.dot(own_t[...], block[...], preferred_element_type=jnp.float32)
        part[stage, 0] = narrow(product[:rows])
        part[stage, 1] = narrow(product[rows:])

    def start(at):
        return send(
            part.at[at, 1 - core], part_in.at[at], (chip_send.at[at], chip_recv.at[at]), sibling
        )

    def cross(at, copy):
        copy.wait_recv()
        chip[at] = narrow(wide(part[at, core]) + wide(part_in[at]))
        return send(chip.at[at], chip_in.at[at], (link_send.at[at], link_recv.at[at]), across)

    def back(at, copy):
        copy.wait_recv()
        dens[at, core] = narrow(wide(chip[at]) + wide(chip_in[at]))
        return send(
            dens.at[at, core], dens.at[at, core], (back_send.at[at], back_recv.at[at]), sibling
        )

    def apply(stage, block, copy):
        copy.wait_recv()
        density = dens[stage].reshape(points, points)
        weight = narrow(wide(kernels[stage]) * wide(density))
        return lax.dot_general(
            block[...], weight, (((1,), (1,)), ((), ())), preferred_element_type=jnp.float32
        )

    if shift:
        target = {"pts": lax.rem(me + shift, blocks)}
        moved = send(swapped, arrived, (shift_sem.at[0], shift_sem.at[1]), target)
    loads[0].wait()
    own_t[...] = own[...].T
    partial(0, own)
    first = start(0)
    if shift:
        first = cross(0, first)
        first = back(0, first)
        loads[1].wait()
        loads[2].wait()
        total[...] = apply(0, own, first)
        moved.wait_recv()
        partial(1, arrived)
        second = start(1)
        second = cross(1, second)
        second = back(1, second)
    else:
        loads[3].wait()
        partial(1, arrived)
        second = start(1)
        first = cross(0, first)
        second = cross(1, second)
        loads[1].wait()
        loads[2].wait()
        first = back(0, first)
        second = back(1, second)
        total[...] = apply(0, own, first)
    out[...] = (total[...] + apply(1, arrived, second)).astype(out.dtype)
    for copy in pending:
        copy.wait_send()


def finish(shift, collective, blocks, groups, orbitals, swapped, self_kernel, pair_kernel):
    bands, points = orbitals.shape
    rows = points // 2
    half = jnp.bfloat16
    dma = pltpu.SemaphoreType.DMA
    return pl.pallas_call(
        functools.partial(finish_kernel, shift, blocks, groups),
        out_shape=jax.ShapeDtypeStruct((bands, points), half),
        in_specs=[pl.BlockSpec(memory_space=pl.ANY)] * 4,
        out_specs=pl.BlockSpec(memory_space=pltpu.VMEM),
        scratch_shapes=[
            pltpu.VMEM((bands, points), half),
            pltpu.VMEM((bands, points), half),
            pltpu.VMEM((2, points, points), half),
            pltpu.VMEM((points, bands), half),
            pltpu.VMEM((2, 2, rows, points), half),
            pltpu.VMEM((2, rows, points), half),
            pltpu.VMEM((2, rows, points), half),
            pltpu.VMEM((2, rows, points), half),
            pltpu.VMEM((2, 2, rows, points), half),
            pltpu.VMEM((bands, points), jnp.float32),
            dma((4,)),
            dma((2,)),
            dma((2,)),
            dma((2,)),
            dma((2,)),
            dma((2,)),
            dma((2,)),
            dma((2,)),
        ],
        compiler_params=pltpu.CompilerParams(
            collective_id=collective, has_side_effects=True, vmem_limit_bytes=VMEM
        ),
    )(orbitals, swapped, self_kernel, pair_kernel)


def per_device(blocks, groups, orbitals, partner, self_kernel, pair_kernel):
    shift = max(blocks // 8, 2)
    pairs = shift // 2
    count = blocks // 4
    round_number = lax.rem(partner[0] + lax.axis_index("pts"), blocks)
    bit = lax.rem(round_number // shift, 2)
    index = round_number // (2 * shift) * pairs + lax.rem(round_number, shift) // 2
    swaps = [
        functools.partial(swap, 2 * shift * (k // pairs) + 2 * (k % pairs) + 1, k, blocks)
        for k in range(count)
    ]
    swapped = lax.switch(index, swaps, orbitals)
    return lax.cond(
        bit == 1,
        functools.partial(finish, shift, count, blocks, groups),
        functools.partial(finish, 0, count + 1, blocks, groups),
        orbitals,
        swapped,
        self_kernel,
        pair_kernel,
    )


def solution(mesh):
    return jax.shard_map(
        functools.partial(per_device, mesh.shape["pts"], mesh.shape["band"]),
        mesh=mesh,
        in_specs=(P("band", "pts"), P("pts"), P("pts", None), P("pts", None)),
        out_specs=P("band", "pts"),
        check_vma=False,
    )
```

```python
import functools

import jax
import jax.numpy as jnp
from jax import lax
from jax.experimental import pallas as pl
from jax.experimental.pallas import tpu as pltpu
from jax.sharding import PartitionSpec as P

MESH = pl.DeviceIdType.MESH
VMEM = 56 * 1024 * 1024


def swap_kernel(round_number, blocks, orbitals, arrived, between, send_sem, recv_sem):
    me = lax.axis_index("pts")
    line = max(blocks // 8, 2)
    partner = lax.rem(round_number + blocks - me, blocks)
    row_mate = partner // line * line + lax.rem(me, line)
    place_mate = me // line * line + lax.rem(partner, line)
    moves = row_mate != me
    bands, points = orbitals.shape
    split = bands // 32 * 16
    width = points // 2
    pieces = [
        (pl.ds(first, size), pl.ds(column * width, width))
        for first, size in ((0, split), (split, bands - split))
        for column in range(2)
    ]
    odd = lax.rem(lax.axis_index("band"), 2) == 1
    ahead = jnp.where(odd, place_mate, row_mate)
    behind = jnp.where(odd, row_mate, place_mate)
    mates = [ahead, behind, ahead, behind]

    barrier = pltpu.get_barrier_semaphore()
    pl.semaphore_signal(barrier, inc=1, device_id={"pts": place_mate}, device_id_type=MESH)

    @pl.when(moves)
    def _():
        pl.semaphore_signal(barrier, inc=1, device_id={"pts": row_mate}, device_id_type=MESH)

    def send(src, dst, piece, semaphore, mate):
        return pltpu.make_async_remote_copy(
            src_ref=src.at[piece],
            dst_ref=dst.at[piece],
            send_sem=send_sem.at[semaphore],
            recv_sem=recv_sem.at[semaphore],
            device_id={"pts": mate},
            device_id_type=MESH,
        )

    count = len(pieces)

    @pl.when(jnp.logical_not(moves))
    def _():
        pl.semaphore_wait(barrier, 1)
        copies = [
            send(orbitals, arrived, piece, count + k, place_mate) for k, piece in enumerate(pieces)
        ]
        for copy in copies:
            copy.start()
        for copy in copies:
            copy.wait()

    @pl.when(moves)
    def _():
        pl.semaphore_wait(barrier, 2)
        firsts = [
            send(orbitals, between, piece, k, mates[k]) for k, piece in enumerate(pieces)
        ]
        seconds = [
            send(between, arrived, piece, count + k, mates[k ^ 1]) for k, piece in enumerate(pieces)
        ]
        for copy in firsts:
            copy.start()
        for first, second in zip(firsts, seconds):
            first.wait_recv()
            second.start()
        for copy in firsts:
            copy.wait_send()
        for copy in seconds:
            copy.wait()


def swap(round_number, collective, blocks, orbitals):
    return pl.pallas_call(
        functools.partial(swap_kernel, round_number, blocks),
        out_shape=jax.ShapeDtypeStruct(orbitals.shape, orbitals.dtype),
        in_specs=[pl.BlockSpec(memory_space=pl.ANY)],
        out_specs=pl.BlockSpec(memory_space=pl.ANY),
        scratch_shapes=[
            pltpu.VMEM(orbitals.shape, orbitals.dtype),
            pltpu.SemaphoreType.DMA((8,)),
            pltpu.SemaphoreType.DMA((8,)),
        ],
        compiler_params=pltpu.CompilerParams(
            collective_id=collective, has_side_effects=True, vmem_limit_bytes=VMEM
        ),
    )(orbitals)


def finish_kernel(
    shift,
    blocks,
    groups,
    orbitals,
    swapped,
    self_kernel,
    pair_kernel,
    out,
    own,
    arrived,
    kernels,
    own_t,
    part,
    part_in,
    chip,
    chip_in,
    dens,
    total,
    local_sem,
    shift_sem,
    chip_send,
    chip_recv,
    link_send,
    link_recv,
    back_send,
    back_recv,
):
    me = lax.axis_index("pts")
    band = lax.axis_index("band")
    core = lax.rem(band, 2)
    sibling = {"band": band + 1 - 2 * core}
    across = {"band": lax.rem(band + 2, groups)}
    points = own.shape[1]
    rows = points // 2

    loads = [
        pltpu.make_async_copy(orbitals, own, local_sem.at[0]),
        pltpu.make_async_copy(self_kernel, kernels.at[0], local_sem.at[1]),
        pltpu.make_async_copy(pair_kernel, kernels.at[1], local_sem.at[2]),
    ]
    if not shift:
        loads.append(pltpu.make_async_copy(swapped, arrived, local_sem.at[3]))
    for load in loads:
        load.start()

    barrier = pltpu.get_barrier_semaphore()
    pl.semaphore_signal(barrier, inc=1, device_id=sibling, device_id_type=MESH)
    pl.semaphore_signal(barrier, inc=1, device_id=across, device_id_type=MESH)
    if shift:
        source = {"pts": lax.rem(me + blocks - shift, blocks)}
        pl.semaphore_signal(barrier, inc=1, device_id=source, device_id_type=MESH)
    if shift:
        pl.semaphore_wait(barrier, 3)

    pending = []

    def send(src, dst, semaphores, target):
        copy = pltpu.make_async_remote_copy(
            src_ref=src,
            dst_ref=dst,
            send_sem=semaphores[0],
            recv_sem=semaphores[1],
            device_id=target,
            device_id_type=MESH,
        )
        copy.start()
        pending.append(copy)
        return copy

    def wide(value):
        return value.astype(jnp.float32)

    def narrow(value):
        return value.astype(jnp.bfloat16)

    def partial(stage, block):
        product = jnp.dot(own_t[...], block[...], preferred_element_type=jnp.float32)
        part[stage, 0] = narrow(product[:rows])
        part[stage, 1] = narrow(product[rows:])

    def start(at):
        return send(
            part.at[at, 1 - core], part_in.at[at], (chip_send.at[at], chip_recv.at[at]), sibling
        )

    def cross(at, copy):
        copy.wait_recv()
        chip[at] = narrow(wide(part[at, core]) + wide(part_in[at]))
        return send(chip.at[at], chip_in.at[at], (link_send.at[at], link_recv.at[at]), across)

    def back(at, copy):
        copy.wait_recv()
        dens[at, core] = narrow(wide(chip[at]) + wide(chip_in[at]))
        return send(
            dens.at[at, core], dens.at[at, core], (back_send.at[at], back_recv.at[at]), sibling
        )

    def apply(stage, block, copy):
        copy.wait_recv()
        density = dens[stage].reshape(points, points)
        weight = narrow(wide(kernels[stage]) * wide(density))
        return lax.dot_general(
            block[...], weight, (((1,), (1,)), ((), ())), preferred_element_type=jnp.float32
        )

    if shift:
        target = {"pts": lax.rem(me + shift, blocks)}
        moved = send(swapped, arrived, (shift_sem.at[0], shift_sem.at[1]), target)
    loads[0].wait()
    own_t[...] = own[...].T
    partial(0, own)
    if not shift:
        loads[3].wait()
        partial(1, arrived)
        pl.semaphore_wait(barrier, 2)
    first = start(0)
    if shift:
        first = cross(0, first)
        first = back(0, first)
        loads[1].wait()
        loads[2].wait()
        total[...] = apply(0, own, first)
        moved.wait_recv()
        partial(1, arrived)
        second = start(1)
        second = cross(1, second)
        second = back(1, second)
    else:
        second = start(1)
        first = cross(0, first)
        second = cross(1, second)
        loads[1].wait()
        loads[2].wait()
        first = back(0, first)
        second = back(1, second)
        total[...] = apply(0, own, first)
    out[...] = (total[...] + apply(1, arrived, second)).astype(out.dtype)
    for copy in pending:
        copy.wait_send()


def finish(shift, collective, blocks, groups, orbitals, swapped, self_kernel, pair_kernel):
    bands, points = orbitals.shape
    rows = points // 2
    half = jnp.bfloat16
    dma = pltpu.SemaphoreType.DMA
    return pl.pallas_call(
        functools.partial(finish_kernel, shift, blocks, groups),
        out_shape=jax.ShapeDtypeStruct((bands, points), half),
        in_specs=[pl.BlockSpec(memory_space=pl.ANY)] * 4,
        out_specs=pl.BlockSpec(memory_space=pltpu.VMEM),
        scratch_shapes=[
            pltpu.VMEM((bands, points), half),
            pltpu.VMEM((bands, points), half),
            pltpu.VMEM((2, points, points), half),
            pltpu.VMEM((points, bands), half),
            pltpu.VMEM((2, 2, rows, points), half),
            pltpu.VMEM((2, rows, points), half),
            pltpu.VMEM((2, rows, points), half),
            pltpu.VMEM((2, rows, points), half),
            pltpu.VMEM((2, 2, rows, points), half),
            pltpu.VMEM((bands, points), jnp.float32),
            dma((4,)),
            dma((2,)),
            dma((2,)),
            dma((2,)),
            dma((2,)),
            dma((2,)),
            dma((2,)),
            dma((2,)),
        ],
        compiler_params=pltpu.CompilerParams(
            collective_id=collective, has_side_effects=True, vmem_limit_bytes=VMEM
        ),
    )(orbitals, swapped, self_kernel, pair_kernel)


def per_device(blocks, groups, orbitals, partner, self_kernel, pair_kernel):
    shift = max(blocks // 8, 2)
    pairs = shift // 2
    count = blocks // 4
    round_number = lax.rem(partner[0] + lax.axis_index("pts"), blocks)
    bit = lax.rem(round_number // shift, 2)
    index = round_number // (2 * shift) * pairs + lax.rem(round_number, shift) // 2
    swaps = [
        functools.partial(swap, 2 * shift * (k // pairs) + 2 * (k % pairs) + 1, k, blocks)
        for k in range(count)
    ]
    swapped = lax.switch(index, swaps, orbitals)
    return lax.cond(
        bit == 1,
        functools.partial(finish, shift, count, blocks, groups),
        functools.partial(finish, 0, count + 1, blocks, groups),
        orbitals,
        swapped,
        self_kernel,
        pair_kernel,
    )


def solution(mesh):
    return jax.shard_map(
        functools.partial(per_device, mesh.shape["pts"], mesh.shape["band"]),
        mesh=mesh,
        in_specs=(P("band", "pts"), P("pts"), P("pts", None), P("pts", None)),
        out_specs=P("band", "pts"),
        check_vma=False,
    )
```

```python
import functools

import jax
import jax.numpy as jnp
from jax import lax
from jax.experimental import pallas as pl
from jax.experimental.pallas import tpu as pltpu
from jax.sharding import PartitionSpec as P

MESH = pl.DeviceIdType.MESH
VMEM = 56 * 1024 * 1024


def swap_kernel(round_number, blocks, orbitals, arrived, between, send_sem, recv_sem):
    me = lax.axis_index("pts")
    line = max(blocks // 8, 2)
    partner = lax.rem(round_number + blocks - me, blocks)
    row_mate = partner // line * line + lax.rem(me, line)
    place_mate = me // line * line + lax.rem(partner, line)
    moves = row_mate != me
    bands, points = orbitals.shape
    split = bands // 32 * 16
    width = points // 2
    pieces = [
        (pl.ds(first, size), pl.ds(column * width, width))
        for first, size in ((0, split), (split, bands - split))
        for column in range(2)
    ]
    odd = lax.rem(lax.axis_index("band"), 2) == 1
    ahead = jnp.where(odd, place_mate, row_mate)
    behind = jnp.where(odd, row_mate, place_mate)
    mates = [ahead, behind, ahead, behind]

    barrier = pltpu.get_barrier_semaphore()
    pl.semaphore_signal(barrier, inc=1, device_id={"pts": place_mate}, device_id_type=MESH)

    @pl.when(moves)
    def _():
        pl.semaphore_signal(barrier, inc=1, device_id={"pts": row_mate}, device_id_type=MESH)

    def send(src, dst, piece, semaphore, mate):
        return pltpu.make_async_remote_copy(
            src_ref=src.at[piece],
            dst_ref=dst.at[piece],
            send_sem=send_sem.at[semaphore],
            recv_sem=recv_sem.at[semaphore],
            device_id={"pts": mate},
            device_id_type=MESH,
        )

    count = len(pieces)

    @pl.when(jnp.logical_not(moves))
    def _():
        pl.semaphore_wait(barrier, 1)
        copies = [
            send(orbitals, arrived, piece, count + k, place_mate) for k, piece in enumerate(pieces)
        ]
        for copy in copies:
            copy.start()
        for copy in copies:
            copy.wait()

    @pl.when(moves)
    def _():
        pl.semaphore_wait(barrier, 2)
        firsts = [
            send(orbitals, between, piece, k, mates[k]) for k, piece in enumerate(pieces)
        ]
        seconds = [
            send(between, arrived, piece, count + k, mates[k ^ 1]) for k, piece in enumerate(pieces)
        ]
        for copy in firsts:
            copy.start()
        for first, second in zip(firsts, seconds):
            first.wait_recv()
            second.start()
        for copy in firsts:
            copy.wait_send()
        for copy in seconds:
            copy.wait()


def swap(round_number, collective, blocks, orbitals):
    return pl.pallas_call(
        functools.partial(swap_kernel, round_number, blocks),
        out_shape=jax.ShapeDtypeStruct(orbitals.shape, orbitals.dtype),
        in_specs=[pl.BlockSpec(memory_space=pl.ANY)],
        out_specs=pl.BlockSpec(memory_space=pl.ANY),
        scratch_shapes=[
            pltpu.VMEM(orbitals.shape, orbitals.dtype),
            pltpu.SemaphoreType.DMA((8,)),
            pltpu.SemaphoreType.DMA((8,)),
        ],
        compiler_params=pltpu.CompilerParams(
            collective_id=collective, has_side_effects=True, vmem_limit_bytes=VMEM
        ),
    )(orbitals)


def finish_kernel(
    shift,
    blocks,
    groups,
    orbitals,
    swapped,
    self_kernel,
    pair_kernel,
    out,
    own,
    arrived,
    kernels,
    own_t,
    part,
    part_in,
    chip,
    chip_in,
    dens,
    total,
    local_sem,
    shift_sem,
    chip_send,
    chip_recv,
    link_send,
    link_recv,
    back_send,
    back_recv,
):
    me = lax.axis_index("pts")
    band = lax.axis_index("band")
    core = lax.rem(band, 2)
    sibling = {"band": band + 1 - 2 * core}
    across = {"band": lax.rem(band + 2, groups)}
    points = own.shape[1]
    rows = points // 2

    loads = [
        pltpu.make_async_copy(orbitals, own, local_sem.at[0]),
        pltpu.make_async_copy(self_kernel, kernels.at[0], local_sem.at[1]),
        pltpu.make_async_copy(pair_kernel, kernels.at[1], local_sem.at[2]),
    ]
    if not shift:
        loads.append(pltpu.make_async_copy(swapped, arrived, local_sem.at[3]))
    for load in loads:
        load.start()

    barrier = pltpu.get_barrier_semaphore()
    pl.semaphore_signal(barrier, inc=1, device_id=sibling, device_id_type=MESH)
    pl.semaphore_signal(barrier, inc=1, device_id=across, device_id_type=MESH)
    if shift:
        source = {"pts": lax.rem(me + blocks - shift, blocks)}
        pl.semaphore_signal(barrier, inc=1, device_id=source, device_id_type=MESH)
    if shift:
        pl.semaphore_wait(barrier, 3)

    pending = []

    def send(src, dst, semaphores, target):
        copy = pltpu.make_async_remote_copy(
            src_ref=src,
            dst_ref=dst,
            send_sem=semaphores[0],
            recv_sem=semaphores[1],
            device_id=target,
            device_id_type=MESH,
        )
        copy.start()
        pending.append(copy)
        return copy

    def wide(value):
        return value.astype(jnp.float32)

    def narrow(value):
        return value.astype(jnp.bfloat16)

    def partial(stage, block, columns):
        product = jnp.dot(own_t[...], block[:, columns], preferred_element_type=jnp.float32)
        part[stage, 0, :, columns] = narrow(product[:rows])
        part[stage, 1, :, columns] = narrow(product[rows:])

    def start(at, stage, columns):
        return send(
            part.at[stage, 1 - core, :, columns],
            part_in.at[stage, :, columns],
            (chip_send.at[at], chip_recv.at[at]),
            sibling,
        )

    def cross(at, stage, columns, copy):
        copy.wait_recv()
        chip[stage, :, columns] = narrow(
            wide(part[stage, core, :, columns]) + wide(part_in[stage, :, columns])
        )
        return send(
            chip.at[stage, :, columns],
            chip_in.at[stage, :, columns],
            (link_send.at[at], link_recv.at[at]),
            across,
        )

    def back(at, stage, columns, copy):
        copy.wait_recv()
        dens[stage, core, :, columns] = narrow(
            wide(chip[stage, :, columns]) + wide(chip_in[stage, :, columns])
        )
        return send(
            dens.at[stage, core, :, columns],
            dens.at[stage, core, :, columns],
            (back_send.at[at], back_recv.at[at]),
            sibling,
        )

    def span(half):
        return pl.ds(pl.multiple_of(half * rows, rows), rows)

    def apply(stage, block, half):
        weight = narrow(wide(kernels[stage, span(half)]) * wide(dens[stage, half]))
        return lax.dot_general(
            block[...], weight, (((1,), (1,)), ((), ())), preferred_element_type=jnp.float32
        )

    def keep(half):
        total[half] = apply(0, own, half)

    def put(half):
        out[:, span(half)] = (total[half] + apply(1, arrived, half)).astype(out.dtype)

    whole = pl.ds(0, points)
    halves = [pl.ds(0, rows), pl.ds(rows, rows)]
    if shift:
        target = {"pts": lax.rem(me + shift, blocks)}
        moved = [
            send(
                swapped.at[:, columns],
                arrived.at[:, columns],
                (shift_sem.at[0, h], shift_sem.at[1, h]),
                target,
            )
            for h, columns in enumerate(halves)
        ]
    loads[0].wait()
    own_t[...] = own[...].T
    partial(0, own, whole)
    if not shift:
        loads[3].wait()
        partial(1, arrived, whole)
        pl.semaphore_wait(barrier, 2)
    first = start(0, 0, whole)
    if shift:
        first = cross(0, 0, whole, first)
        first = back(0, 0, whole, first)
        loads[1].wait()
        loads[2].wait()
        keep(core)
        first.wait_recv()
        seconds = []
        for h, columns in enumerate(halves):
            moved[h].wait_recv()
            partial(1, arrived, columns)
            seconds.append(start(1 + h, 1, columns))
            if h == 0:
                keep(1 - core)
        seconds = [cross(1 + h, 1, halves[h], copy) for h, copy in enumerate(seconds)]
        seconds = [back(1 + h, 1, halves[h], copy) for h, copy in enumerate(seconds)]
    else:
        second = start(1, 1, whole)
        first = cross(0, 0, whole, first)
        second = cross(1, 1, whole, second)
        loads[1].wait()
        loads[2].wait()
        first = back(0, 0, whole, first)
        seconds = [back(1, 1, whole, second)]
        keep(core)
        first.wait_recv()
        keep(1 - core)
    put(core)
    for copy in seconds:
        copy.wait_recv()
    put(1 - core)
    for copy in pending:
        copy.wait_send()


def finish(shift, collective, blocks, groups, orbitals, swapped, self_kernel, pair_kernel):
    bands, points = orbitals.shape
    rows = points // 2
    half = jnp.bfloat16
    dma = pltpu.SemaphoreType.DMA
    return pl.pallas_call(
        functools.partial(finish_kernel, shift, blocks, groups),
        out_shape=jax.ShapeDtypeStruct((bands, points), half),
        in_specs=[pl.BlockSpec(memory_space=pl.ANY)] * 4,
        out_specs=pl.BlockSpec(memory_space=pltpu.VMEM),
        scratch_shapes=[
            pltpu.VMEM((bands, points), half),
            pltpu.VMEM((bands, points), half),
            pltpu.VMEM((2, points, points), half),
            pltpu.VMEM((points, bands), half),
            pltpu.VMEM((2, 2, rows, points), half),
            pltpu.VMEM((2, rows, points), half),
            pltpu.VMEM((2, rows, points), half),
            pltpu.VMEM((2, rows, points), half),
            pltpu.VMEM((2, 2, rows, points), half),
            pltpu.VMEM((2, bands, rows), jnp.float32),
            dma((4,)),
            dma((2, 2)),
            dma((3,)),
            dma((3,)),
            dma((3,)),
            dma((3,)),
            dma((3,)),
            dma((3,)),
        ],
        compiler_params=pltpu.CompilerParams(
            collective_id=collective, has_side_effects=True, vmem_limit_bytes=VMEM
        ),
    )(orbitals, swapped, self_kernel, pair_kernel)


def per_device(blocks, groups, orbitals, partner, self_kernel, pair_kernel):
    shift = max(blocks // 8, 2)
    pairs = shift // 2
    count = blocks // 4

    def upper(low):
        return low // pairs if pairs > 1 else 0

    round_number = lax.rem(partner[0] + lax.axis_index("pts"), blocks)
    low = lax.rem(round_number, shift)
    high = round_number // shift
    bit = lax.rem(high + upper(low), 2)
    index = lax.rem(high + blocks // shift - bit, blocks // shift) // 2 * pairs + low // 2
    swaps = []
    for k in range(count):
        base_low = 2 * (k % pairs) + 1
        base_high = 2 * (k // pairs) + upper(base_low)
        swaps.append(functools.partial(swap, shift * base_high + base_low, k, blocks))
    swapped = lax.switch(index, swaps, orbitals)
    return lax.cond(
        bit == 1,
        functools.partial(finish, shift, count, blocks, groups),
        functools.partial(finish, 0, count + 1, blocks, groups),
        orbitals,
        swapped,
        self_kernel,
        pair_kernel,
    )


def solution(mesh):
    return jax.shard_map(
        functools.partial(per_device, mesh.shape["pts"], mesh.shape["band"]),
        mesh=mesh,
        in_specs=(P("band", "pts"), P("pts"), P("pts", None), P("pts", None)),
        out_specs=P("band", "pts"),
        check_vma=False,
    )
```

```python
import functools

import jax
import jax.numpy as jnp
from jax import lax
from jax.experimental import pallas as pl
from jax.experimental.pallas import tpu as pltpu
from jax.sharding import PartitionSpec as P

MESH = pl.DeviceIdType.MESH
VMEM = 56 * 1024 * 1024


def swap_kernel(round_number, blocks, orbitals, arrived, between, send_sem, recv_sem):
    me = lax.axis_index("pts")
    line = max(blocks // 8, 2)
    partner = lax.rem(round_number + blocks - me, blocks)
    row_mate = partner // line * line + lax.rem(me, line)
    place_mate = me // line * line + lax.rem(partner, line)
    moves = row_mate != me
    bands, points = orbitals.shape
    split = bands // 32 * 16
    width = points // 2
    pieces = [
        (pl.ds(first, size), pl.ds(column * width, width))
        for first, size in ((0, split), (split, bands - split))
        for column in range(2)
    ]
    odd = lax.rem(lax.axis_index("band"), 2) == 1
    ahead = jnp.where(odd, place_mate, row_mate)
    behind = jnp.where(odd, row_mate, place_mate)
    mates = [ahead, behind, ahead, behind]

    barrier = pltpu.get_barrier_semaphore()
    pl.semaphore_signal(barrier, inc=1, device_id={"pts": place_mate}, device_id_type=MESH)

    @pl.when(moves)
    def _():
        pl.semaphore_signal(barrier, inc=1, device_id={"pts": row_mate}, device_id_type=MESH)

    def send(src, dst, piece, semaphore, mate):
        return pltpu.make_async_remote_copy(
            src_ref=src.at[piece],
            dst_ref=dst.at[piece],
            send_sem=send_sem.at[semaphore],
            recv_sem=recv_sem.at[semaphore],
            device_id={"pts": mate},
            device_id_type=MESH,
        )

    count = len(pieces)

    @pl.when(jnp.logical_not(moves))
    def _():
        pl.semaphore_wait(barrier, 1)
        copies = [
            send(orbitals, arrived, piece, count + k, place_mate) for k, piece in enumerate(pieces)
        ]
        for copy in copies:
            copy.start()
        for copy in copies:
            copy.wait()

    @pl.when(moves)
    def _():
        pl.semaphore_wait(barrier, 2)
        firsts = [
            send(orbitals, between, piece, k, mates[k]) for k, piece in enumerate(pieces)
        ]
        seconds = [
            send(between, arrived, piece, count + k, mates[k ^ 1]) for k, piece in enumerate(pieces)
        ]
        for copy in firsts:
            copy.start()
        for first, second in zip(firsts, seconds):
            first.wait_recv()
            second.start()
        for copy in firsts:
            copy.wait_send()
        for copy in seconds:
            copy.wait()


def swap(round_number, collective, blocks, orbitals):
    return pl.pallas_call(
        functools.partial(swap_kernel, round_number, blocks),
        out_shape=jax.ShapeDtypeStruct(orbitals.shape, orbitals.dtype),
        in_specs=[pl.BlockSpec(memory_space=pl.ANY)],
        out_specs=pl.BlockSpec(memory_space=pl.ANY),
        scratch_shapes=[
            pltpu.VMEM(orbitals.shape, orbitals.dtype),
            pltpu.SemaphoreType.DMA((8,)),
            pltpu.SemaphoreType.DMA((8,)),
        ],
        compiler_params=pltpu.CompilerParams(
            collective_id=collective, has_side_effects=True, vmem_limit_bytes=VMEM
        ),
    )(orbitals)


def finish_kernel(
    shift,
    blocks,
    groups,
    orbitals,
    swapped,
    self_kernel,
    pair_kernel,
    out,
    own,
    arrived,
    kernels,
    own_t,
    part,
    part_in,
    chip,
    chip_in,
    dens,
    total,
    local_sem,
    shift_sem,
    chip_send,
    chip_recv,
    link_send,
    link_recv,
    back_send,
    back_recv,
):
    me = lax.axis_index("pts")
    band = lax.axis_index("band")
    core = lax.rem(band, 2)
    sibling = {"band": band + 1 - 2 * core}
    across = {"band": lax.rem(band + 2, groups)}
    points = own.shape[1]
    rows = points // 2

    loads = [
        pltpu.make_async_copy(orbitals, own, local_sem.at[0]),
        pltpu.make_async_copy(self_kernel, kernels.at[0], local_sem.at[1]),
        pltpu.make_async_copy(pair_kernel, kernels.at[1], local_sem.at[2]),
    ]
    if not shift:
        loads.append(pltpu.make_async_copy(swapped, arrived, local_sem.at[3]))
    for load in loads:
        load.start()

    barrier = pltpu.get_barrier_semaphore()
    pl.semaphore_signal(barrier, inc=1, device_id=sibling, device_id_type=MESH)
    pl.semaphore_signal(barrier, inc=1, device_id=across, device_id_type=MESH)
    if shift:
        source = {"pts": lax.rem(me + shift, blocks)}
        pl.semaphore_signal(barrier, inc=1, device_id=source, device_id_type=MESH)
    if shift:
        pl.semaphore_wait(barrier, 3)

    pending = []

    def send(src, dst, semaphores, target):
        copy = pltpu.make_async_remote_copy(
            src_ref=src,
            dst_ref=dst,
            send_sem=semaphores[0],
            recv_sem=semaphores[1],
            device_id=target,
            device_id_type=MESH,
        )
        copy.start()
        pending.append(copy)
        return copy

    def wide(value):
        return value.astype(jnp.float32)

    def narrow(value):
        return value.astype(jnp.bfloat16)

    def partial(stage, block, columns):
        product = jnp.dot(own_t[...], block[:, columns], preferred_element_type=jnp.float32)
        part[stage, 0, :, columns] = narrow(product[:rows])
        part[stage, 1, :, columns] = narrow(product[rows:])

    def start(at, stage, columns):
        return send(
            part.at[stage, 1 - core, :, columns],
            part_in.at[stage, :, columns],
            (chip_send.at[at], chip_recv.at[at]),
            sibling,
        )

    def cross(at, stage, columns, copy):
        copy.wait_recv()
        chip[stage, :, columns] = narrow(
            wide(part[stage, core, :, columns]) + wide(part_in[stage, :, columns])
        )
        return send(
            chip.at[stage, :, columns],
            chip_in.at[stage, :, columns],
            (link_send.at[at], link_recv.at[at]),
            across,
        )

    def back(at, stage, columns, copy):
        copy.wait_recv()
        dens[stage, core, :, columns] = narrow(
            wide(chip[stage, :, columns]) + wide(chip_in[stage, :, columns])
        )
        return send(
            dens.at[stage, core, :, columns],
            dens.at[stage, core, :, columns],
            (back_send.at[at], back_recv.at[at]),
            sibling,
        )

    def span(half):
        return pl.ds(pl.multiple_of(half * rows, rows), rows)

    def apply(stage, block, half):
        weight = narrow(wide(kernels[stage, span(half)]) * wide(dens[stage, half]))
        return lax.dot_general(
            block[...], weight, (((1,), (1,)), ((), ())), preferred_element_type=jnp.float32
        )

    def keep(half):
        total[half] = apply(0, own, half)

    def put(half):
        out[:, span(half)] = (total[half] + apply(1, arrived, half)).astype(out.dtype)

    whole = pl.ds(0, points)
    halves = [pl.ds(0, rows), pl.ds(rows, rows)]
    if shift:
        target = {"pts": lax.rem(me + blocks - shift, blocks)}
        moved = [
            send(
                swapped.at[:, columns],
                arrived.at[:, columns],
                (shift_sem.at[0, h], shift_sem.at[1, h]),
                target,
            )
            for h, columns in enumerate(halves)
        ]
    loads[0].wait()
    own_t[...] = own[...].T
    partial(0, own, whole)
    if not shift:
        loads[3].wait()
        partial(1, arrived, whole)
        pl.semaphore_wait(barrier, 2)
    first = start(0, 0, whole)
    if shift:
        first = cross(0, 0, whole, first)
        first = back(0, 0, whole, first)
        loads[1].wait()
        loads[2].wait()
        keep(core)
        first.wait_recv()
        seconds = []
        for h, columns in enumerate(halves):
            moved[h].wait_recv()
            partial(1, arrived, columns)
            seconds.append(start(1 + h, 1, columns))
            if h == 0:
                keep(1 - core)
        seconds = [cross(1 + h, 1, halves[h], copy) for h, copy in enumerate(seconds)]
        seconds = [back(1 + h, 1, halves[h], copy) for h, copy in enumerate(seconds)]
    else:
        second = start(1, 1, whole)
        first = cross(0, 0, whole, first)
        second = cross(1, 1, whole, second)
        loads[1].wait()
        loads[2].wait()
        first = back(0, 0, whole, first)
        seconds = [back(1, 1, whole, second)]
        keep(core)
        first.wait_recv()
        keep(1 - core)
    put(core)
    for copy in seconds:
        copy.wait_recv()
    put(1 - core)
    for copy in pending:
        copy.wait_send()


def finish(shift, collective, blocks, groups, orbitals, swapped, self_kernel, pair_kernel):
    bands, points = orbitals.shape
    rows = points // 2
    half = jnp.bfloat16
    dma = pltpu.SemaphoreType.DMA
    return pl.pallas_call(
        functools.partial(finish_kernel, shift, blocks, groups),
        out_shape=jax.ShapeDtypeStruct((bands, points), half),
        in_specs=[pl.BlockSpec(memory_space=pl.ANY)] * 4,
        out_specs=pl.BlockSpec(memory_space=pltpu.VMEM),
        scratch_shapes=[
            pltpu.VMEM((bands, points), half),
            pltpu.VMEM((bands, points), half),
            pltpu.VMEM((2, points, points), half),
            pltpu.VMEM((points, bands), half),
            pltpu.VMEM((2, 2, rows, points), half),
            pltpu.VMEM((2, rows, points), half),
            pltpu.VMEM((2, rows, points), half),
            pltpu.VMEM((2, rows, points), half),
            pltpu.VMEM((2, 2, rows, points), half),
            pltpu.VMEM((2, bands, rows), jnp.float32),
            dma((4,)),
            dma((2, 2)),
            dma((3,)),
            dma((3,)),
            dma((3,)),
            dma((3,)),
            dma((3,)),
            dma((3,)),
        ],
        compiler_params=pltpu.CompilerParams(
            collective_id=collective, has_side_effects=True, vmem_limit_bytes=VMEM
        ),
    )(orbitals, swapped, self_kernel, pair_kernel)


def per_device(blocks, groups, orbitals, partner, self_kernel, pair_kernel):
    shift = max(blocks // 8, 2)
    pairs = shift // 2
    count = blocks // 4

    def upper(low):
        return low // pairs if pairs > 1 else 0

    round_number = lax.rem(partner[0] + lax.axis_index("pts"), blocks)
    low = lax.rem(round_number, shift)
    high = round_number // shift
    bit = lax.rem(high + upper(low), 2)
    index = lax.rem(high + bit, blocks // shift) // 2 * pairs + low // 2
    swaps = []
    for k in range(count):
        base_low = 2 * (k % pairs) + 1
        base_high = 2 * (k // pairs) + upper(base_low)
        swaps.append(functools.partial(swap, shift * base_high + base_low, k, blocks))
    swapped = lax.switch(index, swaps, orbitals)
    return lax.cond(
        bit == 1,
        functools.partial(finish, shift, count, blocks, groups),
        functools.partial(finish, 0, count + 1, blocks, groups),
        orbitals,
        swapped,
        self_kernel,
        pair_kernel,
    )


def solution(mesh):
    return jax.shard_map(
        functools.partial(per_device, mesh.shape["pts"], mesh.shape["band"]),
        mesh=mesh,
        in_specs=(P("band", "pts"), P("pts"), P("pts", None), P("pts", None)),
        out_specs=P("band", "pts"),
        check_vma=False,
    )
```

```python
import functools

import jax
import jax.numpy as jnp
from jax import lax
from jax.experimental import pallas as pl
from jax.experimental.pallas import tpu as pltpu
from jax.sharding import PartitionSpec as P

MESH = pl.DeviceIdType.MESH
VMEM = 56 * 1024 * 1024


def swap_kernel(round_number, blocks, orbitals, arrived, between, send_sem, recv_sem):
    me = lax.axis_index("pts")
    line = max(blocks // 8, 2)
    partner = lax.rem(round_number + blocks - me, blocks)
    row_mate = partner // line * line + lax.rem(me, line)
    place_mate = me // line * line + lax.rem(partner, line)
    moves = row_mate != me
    bands, points = orbitals.shape
    split = bands // 32 * 16
    width = points // 2
    pieces = [
        (pl.ds(first, size), pl.ds(column * width, width))
        for first, size in ((0, split), (split, bands - split))
        for column in range(2)
    ]
    odd = lax.rem(lax.axis_index("band"), 2) == 1
    ahead = jnp.where(odd, place_mate, row_mate)
    behind = jnp.where(odd, row_mate, place_mate)
    mates = [ahead, behind, ahead, behind]

    barrier = pltpu.get_barrier_semaphore()
    pl.semaphore_signal(barrier, inc=1, device_id={"pts": place_mate}, device_id_type=MESH)

    @pl.when(moves)
    def _():
        pl.semaphore_signal(barrier, inc=1, device_id={"pts": row_mate}, device_id_type=MESH)

    def send(src, dst, piece, semaphore, mate):
        return pltpu.make_async_remote_copy(
            src_ref=src.at[piece],
            dst_ref=dst.at[piece],
            send_sem=send_sem.at[semaphore],
            recv_sem=recv_sem.at[semaphore],
            device_id={"pts": mate},
            device_id_type=MESH,
        )

    count = len(pieces)

    @pl.when(jnp.logical_not(moves))
    def _():
        pl.semaphore_wait(barrier, 1)
        copies = [
            send(orbitals, arrived, piece, count + k, place_mate) for k, piece in enumerate(pieces)
        ]
        for copy in copies:
            copy.start()
        for copy in copies:
            copy.wait()

    @pl.when(moves)
    def _():
        pl.semaphore_wait(barrier, 2)
        firsts = [
            send(orbitals, between, piece, k, mates[k]) for k, piece in enumerate(pieces)
        ]
        seconds = [
            send(between, arrived, piece, count + k, mates[k ^ 1]) for k, piece in enumerate(pieces)
        ]
        for copy in firsts:
            copy.start()
        for first, second in zip(firsts, seconds):
            first.wait_recv()
            second.start()
        for copy in firsts:
            copy.wait_send()
        for copy in seconds:
            copy.wait()


def swap(round_number, collective, blocks, orbitals):
    return pl.pallas_call(
        functools.partial(swap_kernel, round_number, blocks),
        out_shape=jax.ShapeDtypeStruct(orbitals.shape, orbitals.dtype),
        in_specs=[pl.BlockSpec(memory_space=pl.ANY)],
        out_specs=pl.BlockSpec(memory_space=pl.ANY),
        scratch_shapes=[
            pltpu.VMEM(orbitals.shape, orbitals.dtype),
            pltpu.SemaphoreType.DMA((8,)),
            pltpu.SemaphoreType.DMA((8,)),
        ],
        compiler_params=pltpu.CompilerParams(
            collective_id=collective, has_side_effects=True, vmem_limit_bytes=VMEM
        ),
    )(orbitals)


def finish_kernel(
    shift,
    blocks,
    groups,
    orbitals,
    swapped,
    self_kernel,
    pair_kernel,
    out,
    own,
    arrived,
    kernels,
    own_t,
    part,
    part_in,
    chip,
    chip_in,
    dens,
    total,
    local_sem,
    shift_sem,
    chip_send,
    chip_recv,
    link_send,
    link_recv,
    back_send,
    back_recv,
):
    me = lax.axis_index("pts")
    band = lax.axis_index("band")
    core = lax.rem(band, 2)
    sibling = {"band": band + 1 - 2 * core}
    across = {"band": lax.rem(band + 2, groups)}
    points = own.shape[1]
    rows = points // 2

    loads = [
        pltpu.make_async_copy(orbitals, own, local_sem.at[0]),
        pltpu.make_async_copy(self_kernel, kernels.at[0], local_sem.at[1]),
        pltpu.make_async_copy(pair_kernel, kernels.at[1], local_sem.at[2]),
    ]
    if not shift:
        loads.append(pltpu.make_async_copy(swapped, arrived, local_sem.at[3]))
    for load in loads:
        load.start()

    barrier = pltpu.get_barrier_semaphore()
    pl.semaphore_signal(barrier, inc=1, device_id=sibling, device_id_type=MESH)
    pl.semaphore_signal(barrier, inc=1, device_id=across, device_id_type=MESH)
    if shift:
        source = {"pts": lax.rem(me + shift, blocks)}
        pl.semaphore_signal(barrier, inc=1, device_id=source, device_id_type=MESH)
    if shift:
        pl.semaphore_wait(barrier, 3)

    pending = []

    def send(src, dst, semaphores, target):
        copy = pltpu.make_async_remote_copy(
            src_ref=src,
            dst_ref=dst,
            send_sem=semaphores[0],
            recv_sem=semaphores[1],
            device_id=target,
            device_id_type=MESH,
        )
        copy.start()
        pending.append(copy)
        return copy

    def wide(value):
        return value.astype(jnp.float32)

    def narrow(value):
        return value.astype(jnp.bfloat16)

    def partial(stage, block, columns):
        product = jnp.dot(own_t[...], block[:, columns], preferred_element_type=jnp.float32)
        part[stage, 0, :, columns] = narrow(product[:rows])
        part[stage, 1, :, columns] = narrow(product[rows:])

    def start(at, stage, columns):
        return send(
            part.at[stage, 1 - core, :, columns],
            part_in.at[stage, :, columns],
            (chip_send.at[at], chip_recv.at[at]),
            sibling,
        )

    def cross(at, stage, columns, copy):
        copy.wait_recv()
        chip[stage, :, columns] = narrow(
            wide(part[stage, core, :, columns]) + wide(part_in[stage, :, columns])
        )
        return send(
            chip.at[stage, :, columns],
            chip_in.at[stage, :, columns],
            (link_send.at[at], link_recv.at[at]),
            across,
        )

    def back(at, stage, columns, copy):
        copy.wait_recv()
        dens[stage, core, :, columns] = narrow(
            wide(chip[stage, :, columns]) + wide(chip_in[stage, :, columns])
        )
        return send(
            dens.at[stage, core, :, columns],
            dens.at[stage, core, :, columns],
            (back_send.at[at], back_recv.at[at]),
            sibling,
        )

    def span(half):
        return pl.ds(pl.multiple_of(half * rows, rows), rows)

    def apply(stage, block, half):
        weight = narrow(wide(kernels[stage, span(half)]) * wide(dens[stage, half]))
        return lax.dot_general(
            block[...], weight, (((1,), (1,)), ((), ())), preferred_element_type=jnp.float32
        )

    def keep(half):
        total[half] = apply(0, own, half)

    def put(half):
        out[:, span(half)] = (total[half] + apply(1, arrived, half)).astype(out.dtype)

    whole = pl.ds(0, points)
    halves = [pl.ds(0, rows), pl.ds(rows, rows)]
    if shift:
        target = {"pts": lax.rem(me + blocks - shift, blocks)}
        moved = [
            send(
                swapped.at[:, columns],
                arrived.at[:, columns],
                (shift_sem.at[0, h], shift_sem.at[1, h]),
                target,
            )
            for h, columns in enumerate(halves)
        ]
    loads[0].wait()
    own_t[...] = own[...].T
    partial(0, own, whole)
    if not shift:
        loads[3].wait()
        partial(1, arrived, whole)
        pl.semaphore_wait(barrier, 2)
    first = start(0, 0, whole)
    if shift:
        first = cross(0, 0, whole, first)
        first = back(0, 0, whole, first)
        loads[1].wait()
        loads[2].wait()
        keep(core)
        first.wait_recv()
        moved[0].wait_recv()
        partial(1, arrived, halves[0])
        left = start(1, 1, halves[0])
        keep(1 - core)
        left = cross(1, 1, halves[0], left)
        moved[1].wait_recv()
        partial(1, arrived, halves[1])
        right = start(2, 1, halves[1])
        left = back(1, 1, halves[0], left)
        right = cross(2, 1, halves[1], right)
        seconds = [left, back(2, 1, halves[1], right)]
    else:
        second = start(1, 1, whole)
        first = cross(0, 0, whole, first)
        second = cross(1, 1, whole, second)
        loads[1].wait()
        loads[2].wait()
        first = back(0, 0, whole, first)
        seconds = [back(1, 1, whole, second)]
        keep(core)
        first.wait_recv()
        keep(1 - core)
    put(core)
    for copy in seconds:
        copy.wait_recv()
    put(1 - core)
    for copy in pending:
        copy.wait_send()


def finish(shift, collective, blocks, groups, orbitals, swapped, self_kernel, pair_kernel):
    bands, points = orbitals.shape
    rows = points // 2
    half = jnp.bfloat16
    dma = pltpu.SemaphoreType.DMA
    return pl.pallas_call(
        functools.partial(finish_kernel, shift, blocks, groups),
        out_shape=jax.ShapeDtypeStruct((bands, points), half),
        in_specs=[pl.BlockSpec(memory_space=pl.ANY)] * 4,
        out_specs=pl.BlockSpec(memory_space=pltpu.VMEM),
        scratch_shapes=[
            pltpu.VMEM((bands, points), half),
            pltpu.VMEM((bands, points), half),
            pltpu.VMEM((2, points, points), half),
            pltpu.VMEM((points, bands), half),
            pltpu.VMEM((2, 2, rows, points), half),
            pltpu.VMEM((2, rows, points), half),
            pltpu.VMEM((2, rows, points), half),
            pltpu.VMEM((2, rows, points), half),
            pltpu.VMEM((2, 2, rows, points), half),
            pltpu.VMEM((2, bands, rows), jnp.float32),
            dma((4,)),
            dma((2, 2)),
            dma((3,)),
            dma((3,)),
            dma((3,)),
            dma((3,)),
            dma((3,)),
            dma((3,)),
        ],
        compiler_params=pltpu.CompilerParams(
            collective_id=collective, has_side_effects=True, vmem_limit_bytes=VMEM
        ),
    )(orbitals, swapped, self_kernel, pair_kernel)


def per_device(blocks, groups, orbitals, partner, self_kernel, pair_kernel):
    shift = max(blocks // 8, 2)
    pairs = shift // 2
    count = blocks // 4

    def upper(low):
        return low // pairs if pairs > 1 else 0

    round_number = lax.rem(partner[0] + lax.axis_index("pts"), blocks)
    low = lax.rem(round_number, shift)
    high = round_number // shift
    bit = lax.rem(high + upper(low), 2)
    index = lax.rem(high + bit, blocks // shift) // 2 * pairs + low // 2
    swaps = []
    for k in range(count):
        base_low = 2 * (k % pairs) + 1
        base_high = 2 * (k // pairs) + upper(base_low)
        swaps.append(functools.partial(swap, shift * base_high + base_low, k, blocks))
    swapped = lax.switch(index, swaps, orbitals)
    return lax.cond(
        bit == 1,
        functools.partial(finish, shift, count, blocks, groups),
        functools.partial(finish, 0, count + 1, blocks, groups),
        orbitals,
        swapped,
        self_kernel,
        pair_kernel,
    )


def solution(mesh):
    return jax.shard_map(
        functools.partial(per_device, mesh.shape["pts"], mesh.shape["band"]),
        mesh=mesh,
        in_specs=(P("band", "pts"), P("pts"), P("pts", None), P("pts", None)),
        out_specs=P("band", "pts"),
        check_vma=False,
    )
```
